512 devices in a mesh: shot: 32 (over y, z_hi), point: 16 (over z_lo, x, core).
Axes of the slice: x: 4, y: 8, z: 8 (z_hi: 4, z_lo: 2; z = z_hi * 2 + z_lo), core: 2. Of those that a mesh axis runs over, the one named last changes fastest.
Arguments:
- traces: bfloat16 [64, 32, 1024], P('shot', 'point'), may hold values from -6 to 6
- panels: bfloat16 [32, 256, 1024], P('point', 'shot'), may hold values from -0.09375 to 0.09375
- aperture: int32 [64, 32], P('shot', 'point'), may hold values 0 or 1
- window_lo: int32 [256, 64], P('point', 'shot'), may hold values from 0 to 255
- window_hi: int32 [256, 64], P('point', 'shot'), may hold values from 512 to 1023
Outputs:
- multiples: bfloat16 [256, 64, 1024], P('point', 'shot')
The draws below stay inside these ranges and needn't reach their ends.
All inputs are finite; a program needn't handle non-finite values. No bound on the sum of `aperture` on one device may be relied on, other than what follows from the above.
Results may differ from the reference program's by a relative error of at most 0.001.
Values may be sent and summed in bfloat16 or wider, within the bound.
A program may use at most 64 MiB of HBM per device.

```python
import jax
import jax.numpy as jnp
from jax import lax

RECEIVERS = 256
SAMPLES = 1024
POINTS = 32
SHOTS = 64


def with_ends(array, rng, least, high):
    index_at = [jax.random.randint(jax.random.fold_in(rng, axis), (), 0, length) for axis, length in enumerate(array.shape)]
    main_axis = array.shape.index(max(array.shape))
    beside = index_at[:main_axis] + [(index_at[main_axis] + 1) % array.shape[main_axis]] + index_at[main_axis + 1:]
    return array.at[tuple(index_at)].set(least).at[tuple(beside)].set(high)


def with_spikes(drawn, rng, source, target, shards_of, factor):
    owner, partner = [(jnp.arange(drawn.shape[axis_at]) // (drawn.shape[axis_at] // shards_of)).reshape([-1 if axis == axis_at else 1 for axis in range(drawn.ndim)]) for axis_at in (source, target)]
    chosen = jax.random.permutation(rng, shards_of)[partner]
    strong = (owner == chosen) | (owner == (partner + shards_of // 2) % shards_of)
    return jnp.where(strong, factor * drawn, drawn)


def steps_of(stream_key, extent, split, smallest, largest):
    def one(dim, parts):
        heights = jax.random.uniform(jax.random.fold_in(jax.random.fold_in(stream_key, 6), dim), (parts,), jnp.float32, smallest / len(split), largest / len(split))
        return jnp.repeat(jnp.exp(heights), extent[dim] // parts).reshape((-1,) + (1,) * (len(extent) - dim - 1))

    factor_of = one(*split[0])
    for cut in split[1:]:
        factor_of = factor_of * one(*cut)
    return factor_of


def normal_values(own_key, shape, width, reach, split=(), kind=jnp.bfloat16):
    loudness = steps_of(own_key, shape, split, -0.22, 0.18) if split else 1.0
    result = jax.random.normal(own_key, shape, jnp.float32) * width * loudness
    return jnp.minimum(jnp.maximum(result, -reach), reach).astype(kind)


def bell_draw_with(stream_key, extent, spread, limit, cuts, heavy, kind=jnp.bfloat16):
    result = spread * jax.random.normal(stream_key, extent, jnp.float32)
    if cuts:
        result = result * steps_of(stream_key, extent, cuts, -0.22, 0.18)
    return jnp.clip(with_spikes(result, jax.random.fold_in(stream_key, 3), *heavy), -limit, limit).astype(kind)


def setup_inputs(seed: int = 0) -> dict:
    key_list = jax.random.split(jax.random.key(seed), 6)
    return {
        "traces": normal_values(key_list[0], (SHOTS, POINTS, SAMPLES), 1.0, 6.0, ((0, 32), (1, 16))),
        "panels": bell_draw_with(key_list[1], (POINTS, RECEIVERS, SAMPLES), (POINTS * SAMPLES // 2) ** -0.5, 0.09375, ((0, 16), (1, 32)), (0, 1, 32, 2.75)),
        "aperture": with_ends((jax.random.randint(key_list[2], (SHOTS, POINTS), 0, 4) < 3).astype(jnp.int32), jax.random.fold_in(key_list[2], 1), 0, 1),
        "window_lo": with_ends(jax.random.randint(key_list[3], (RECEIVERS, SHOTS), 0, SAMPLES // 4), jax.random.fold_in(key_list[3], 1), 0, (SAMPLES // 4) - 1).astype(jnp.int32),
        "window_hi": with_ends(jax.random.randint(key_list[4], (RECEIVERS, SHOTS), SAMPLES // 2, SAMPLES), jax.random.fold_in(key_list[4], 1), SAMPLES // 2, SAMPLES - 1).astype(jnp.int32),
    }


def toeplitz(series):
    count = series.shape[-1]
    padded = jnp.concatenate([series, jnp.zeros_like(series)], -1)
    tiled_flat = jnp.tile(padded, (1, count))[:, :count * (2 * count - 1)]
    return tiled_flat.reshape(series.shape[0], count, 2 * count - 1)[:, :, :count]


def window_weights(window_lo, window_hi, length):
    sample_axis = jnp.arange(length).astype(jnp.float32)[None, None, :]
    lower = window_lo.astype(jnp.float32)[:, :, None]
    upper = window_hi.astype(jnp.float32)[:, :, None]
    rising = jnp.clip((sample_axis - lower + 32.0) / 32.0, 0.0, 1.0)
    falling = jnp.clip((upper - sample_axis) / 32.0, 0.0, 1.0)
    return rising * falling


def reference(traces, panels, aperture, window_lo, window_hi):
    masked = traces * aperture[:, :, None].astype(traces.dtype)

    def one_point(point, total_sum):
        series = lax.dynamic_index_in_dim(masked, point, 1, keepdims=False)
        kernel = toeplitz(series).astype(jnp.float32)
        panel_rows = lax.dynamic_index_in_dim(panels, point, 0, keepdims=False).astype(jnp.float32)
        return total_sum + jnp.einsum("ru,sut->rst", panel_rows, kernel)

    initial = jnp.zeros((panels.shape[1], traces.shape[0], traces.shape[2]), jnp.float32)
    predicted = lax.fori_loop(0, panels.shape[0], one_point, initial)
    weights = window_weights(window_lo, window_hi, traces.shape[2])
    return (weights * predicted).astype(jnp.bfloat16)
```

```python
import jax
import jax.numpy as jnp
from jax import lax
from jax.experimental import pallas as pl
from jax.experimental.pallas import tpu as pltpu
from jax.sharding import PartitionSpec as P

F32, BF16 = jnp.float32, jnp.bfloat16
MESH = pl.DeviceIdType.MESH


def device(y, zh, zl, x, core):
    return (y * 4 + zh, (zl * 4 + x) * 2 + core)


def lane_index(rows):
    return lax.broadcasted_iota(jnp.int32, (rows, 128), 1)


def spread_panels(panel_in, left, g):
    for first in (0, 4):
        blocks = [
            [panel_in[g, b, :, q * 128 : (q + 1) * 128].astype(F32) for b in range(8)]
            for q in range(first, first + 4)
        ]
        rows = [jnp.concatenate([b[p][:8] for b in blocks], 0) for p in range(8)]
        rows += [jnp.concatenate([b[p][8:] for b in blocks], 0) for p in range(8)]
        lane = lane_index(32)
        for bit in (1, 2, 4, 8):
            low = (lane & bit) == 0
            new = list(rows)
            for p in range(16):
                if not p & bit:
                    lo, hi = rows[p], rows[p | bit]
                    new[p] = jnp.where(low, lo, pltpu.roll(hi, bit, 1))
                    new[p | bit] = jnp.where(low, pltpu.roll(lo, 128 - bit, 1), hi)
            rows = new
        for i in range(4):
            q = first + i
            at = ((q // 2) * 4 + g * 2 + q % 2) * 128
            left[:, at : at + 128] = jnp.concatenate([v[8 * i : 8 * i + 8] for v in rows], 0).astype(BF16)


def shift_traces(wide, right, slot, s):
    lane = lane_index(16)

    def one(g, carry):
        base = g * 256 + s * 16
        tiles = [
            jnp.concatenate([wide[pl.ds(base + p * 8 + q, 8, stride=32), :] for p in range(2)], 0)
            for q in range(8)
        ]
        for m in range(8):
            turned = [pltpu.roll(v, 16 * m, 1) if m else v for v in tiles]
            for q in range(8):
                value = turned[q]
                if m:
                    value = jnp.where(lane < 16 * m, turned[q - 1] if q else 0.0, value)
                value = value.astype(BF16)
                for h in range(2):
                    k = q + h
                    if k < 8:
                        row = pl.multiple_of((3 - k // 2) * 512 + g * 256 + h * 128 + m * 16, 16)
                        right[slot, pl.ds(row, 16), (k % 2) * 128 : (k % 2) * 128 + 128] = value
        return carry

    lax.fori_loop(0, 2, one, 0)


def convolve(left, right, slot):
    tiles = []
    for n in range(4):
        z = jnp.dot(
            left[:, : (n + 1) * 512], right[slot, (3 - n) * 512 :, :], preferred_element_type=F32
        )
        tiles += [z[:, :128], z[:, 128:]]
    for k in (8, 4, 2, 1):
        lane = lane_index(8 * k)
        turned = [pltpu.roll(z[k * 8 :], k, 1) for z in tiles]
        tiles = [
            z[: k * 8] + jnp.where(lane < k, turned[q - 1] if q else 0.0, turned[q])
            for q, z in enumerate(tiles)
        ]
    return tiles


def weigh(tiles, lower, upper):
    out = []
    for q, z in enumerate(tiles):
        t = (lane_index(8) + 128 * q).astype(F32)
        rising = jnp.clip((t - lower + 32.0) / 32.0, 0.0, 1.0)
        falling = jnp.clip((upper - t) / 32.0, 0.0, 1.0)
        out.append(rising * falling * z)
    return jnp.concatenate(out, 1)


def kernel(
    panels, traces, aperture, lo, hi, out,
    trace_raw, aperture_raw, lo_raw, hi_raw, trace_wide, trace_out, window_out,
    panel_in, trace_in, window_in, wide, left, right, result_out,
    local_sem, panel_send, panel_recv, pass_send, pass_recv,
    trace_send, trace_recv, window_send, window_recv, result_send, result_recv,
):
    shot, point = lax.axis_index("shot"), lax.axis_index("point")
    y, zh = shot // 4, shot % 4
    zl, x, core = point // 8, (point // 2) % 4, point % 2
    z = zh * 2 + zl
    half = zh // 2
    place = zl * 4 + x

    def start(source, target, send, recv, to):
        pltpu.make_async_remote_copy(
            src_ref=source, dst_ref=target, send_sem=send, recv_sem=recv, device_id=to, device_id_type=MESH
        ).start()

    def landed(ref, sem):
        pltpu.make_async_copy(ref, ref, sem).wait()

    loads = [
        pltpu.make_async_copy(source, target, local_sem.at[i])
        for i, (source, target) in enumerate(
            [(traces, trace_raw), (aperture, aperture_raw), (lo, lo_raw), (hi, hi_raw)]
        )
    ]
    for load in loads:
        load.start()

    barrier = pltpu.get_barrier_semaphore()

    def greet(to):
        pl.semaphore_signal(barrier, inc=1, device_id=to, device_id_type=MESH)

    def greet_traces(i, carry):
        greet(device(y, core * 2 + i // 16, (i // 8) % 2, (i // 2) % 4, i % 2))
        return carry

    def greet_panels(i, carry):
        greet(device(place, zh, i // 4, i % 4, core))
        return carry

    lax.fori_loop(0, 32, greet_traces, 0)
    lax.fori_loop(0, 8, greet_panels, 0)
    for i in range(2):
        greet(device(y, core * 2 + i, zl, x, half))
    greet(device(y, zh, zl, x, 1 - core))

    for load in loads:
        load.wait()
    for s in range(2):
        row = trace_raw[s].astype(F32)
        for p in range(2):
            kept = row[p : p + 1, :] * aperture_raw[s : s + 1, p : p + 1].astype(F32)
            for q in range(8):
                trace_wide[s * 16 + p * 8 + q : s * 16 + p * 8 + q + 1, :] = kept[:, q * 128 : (q + 1) * 128]
    trace_out[...] = trace_wide[...].astype(BF16)
    window_out[:, 0:2] = lo_raw[...].astype(F32)
    window_out[:, 2:4] = hi_raw[...].astype(F32)
    for slot in range(4):
        for g in range(2):
            right[slot, 1536 + g * 256 + 128 : 1536 + g * 256 + 256, 0:128] = jnp.zeros((128, 128), BF16)

    pl.semaphore_wait(barrier, 43)

    mine = (y // 4 == zl) & (y % 4 == x)

    def send_panel(i, carry):
        k = 4 + ((i + 1) // 2) * (2 * ((i + 1) % 2) - 1)
        start(
            panels, panel_in.at[0, place], panel_send, panel_recv.at[place],
            device((y + k) % 8, zh, y // 4, y % 4, core),
        )
        return carry

    lax.fori_loop(0, 7, send_panel, 0)

    @pl.when(mine)
    def _():
        pltpu.make_async_copy(panels, panel_in.at[0, place], panel_recv.at[place]).start()

    @pl.when(jnp.logical_not(mine))
    def _():
        start(
            panels, panel_in.at[0, place], panel_send, panel_recv.at[place], device(y, zh, y // 4, y % 4, core)
        )

    trace_slot = (zh % 2) * 16 + ((core + half) % 2) * 8 + place
    trace_sem = trace_recv.at[zh % 2]
    trace_target = trace_in.at[trace_slot]

    def send_trace(i, carry):
        o = i // 4
        dz = 4 + ((o + 1) // 2) * (2 * ((o + 1) % 2) - 1)
        to = (z + dz) % 8
        start(
            trace_out, trace_target, trace_send, trace_sem, device(y, to // 2, to % 2, (x + 3 - i % 4) % 4, half)
        )
        return carry

    lax.fori_loop(0, 31, send_trace, 0)

    @pl.when(core == half)
    def _():
        pltpu.make_async_copy(trace_out, trace_target, trace_sem).start()

    @pl.when(core != half)
    def _():
        start(trace_out, trace_target, trace_send, trace_sem, device(y, zh, zl, x, half))

    for i in range(2):
        rows = window_out.at[pl.ds(i * 8, 8)]
        to = core * 2 + i
        same = (core == half) & (zh % 2 == i)
        target, sem = window_in.at[zh % 2], window_recv.at[zh % 2]

        @pl.when(same)
        def _():
            pltpu.make_async_copy(rows, target, sem).start()

        @pl.when(jnp.logical_not(same))
        def _():
            start(rows, target, window_send.at[i], sem, device(y, to, zl, x, half))

    for b in range(8):
        landed(panel_in.at[0, b], panel_recv.at[b])
        start(
            panel_in.at[0, b], panel_in.at[1, b], pass_send, pass_recv, device(y, zh, zl, x, 1 - core)
        )
    spread_panels(panel_in, left, 0)
    for part in range(2):
        landed(trace_in.at[pl.ds(part * 16, 16)], trace_recv.at[part])
        wide[...] = trace_in[part * 16 : part * 16 + 16].reshape(512, 128).astype(F32)
        for s in range(2):
            shift_traces(wide, right, part * 2 + s, s)
    landed(panel_in.at[1], pass_recv)
    spread_panels(panel_in, left, 1)
    for part in range(2):
        landed(window_in.at[part], window_recv.at[part])
        for s in range(2):
            value = weigh(
                convolve(left, right, part * 2 + s),
                window_in[part, :, s : s + 1],
                window_in[part, :, 2 + s : 3 + s],
            )
            wide_rows = value.astype(BF16)
            result_out[part, s * 8 : s * 8 + 8, :] = wide_rows
        same = (core == half) & (zh % 2 == part)
        target, sem = out.at[zh % 2], result_recv.at[zh % 2]

        @pl.when(same)
        def _():
            pltpu.make_async_copy(result_out.at[part], target, sem).start()

        @pl.when(jnp.logical_not(same))
        def _():
            start(
                result_out.at[part], target, result_send.at[part], sem, device(y, core * 2 + part, zl, x, half)
            )

    for part in range(2):
        landed(out.at[part], result_recv.at[part])

    @pl.when(mine)
    def _():
        landed(panel_in.at[0, pl.ds(0, 7)], panel_send)

    @pl.when(jnp.logical_not(mine))
    def _():
        landed(panel_in.at[0], panel_send)

    @pl.when(core == half)
    def _():
        landed(trace_in.at[pl.ds(0, 31)], trace_send)

    @pl.when(core != half)
    def _():
        landed(trace_in, trace_send)

    landed(panel_in.at[1], pass_send)
    for i in range(2):
        same = (core == half) & (zh % 2 == i)

        @pl.when(jnp.logical_not(same))
        def _():
            landed(window_in.at[i], window_send.at[i])
            landed(result_out.at[i], result_send.at[i])


def body(traces, panels, aperture, window_lo, window_hi):
    anywhere = pl.BlockSpec(memory_space=pl.ANY)
    out = pl.pallas_call(
        kernel,
        out_shape=jax.ShapeDtypeStruct((2, 16, 1024), BF16),
        in_specs=[anywhere] * 5,
        out_specs=pl.BlockSpec(memory_space=pltpu.VMEM),
        scratch_shapes=[
            pltpu.VMEM((2, 2, 1024), BF16),
            pltpu.VMEM((2, 2), jnp.int32),
            pltpu.VMEM((16, 2), jnp.int32),
            pltpu.VMEM((16, 2), jnp.int32),
            pltpu.VMEM((32, 128), F32),
            pltpu.VMEM((32, 128), BF16),
            pltpu.VMEM((16, 128), F32),
            pltpu.VMEM((2, 8, 16, 1024), BF16),
            pltpu.VMEM((32, 32, 128), BF16),
            pltpu.VMEM((2, 8, 128), F32),
            pltpu.VMEM((512, 128), F32),
            pltpu.VMEM((128, 2048), BF16),
            pltpu.VMEM((4, 2048, 256), BF16),
            pltpu.VMEM((2, 16, 1024), BF16),
            pltpu.SemaphoreType.DMA((4,)),
            pltpu.SemaphoreType.DMA,
            pltpu.SemaphoreType.DMA((8,)),
            pltpu.SemaphoreType.DMA,
            pltpu.SemaphoreType.DMA,
            pltpu.SemaphoreType.DMA,
            pltpu.SemaphoreType.DMA((2,)),
            pltpu.SemaphoreType.DMA((2,)),
            pltpu.SemaphoreType.DMA((2,)),
            pltpu.SemaphoreType.DMA((2,)),
            pltpu.SemaphoreType.DMA((2,)),
        ],
        compiler_params=pltpu.CompilerParams(
            collective_id=0, has_side_effects=True, vmem_limit_bytes=40 << 20
        ),
    )(panels.reshape(16, 1024), traces, aperture, window_lo, window_hi)
    return out.reshape(2, 2, 8, 1024).transpose(0, 2, 1, 3).reshape(16, 2, 1024)


def solution(mesh):
    in_specs = (
        P("shot", "point", None),
        P("point", "shot", None),
        P("shot", "point"),
        P("point", "shot"),
        P("point", "shot"),
    )
    out_specs = P("point", "shot", None)
    return jax.shard_map(body, mesh=mesh, in_specs=in_specs, out_specs=out_specs, check_vma=False)
```

```python
import jax
import jax.numpy as jnp
from jax import lax
from jax.experimental import pallas as pl
from jax.experimental.pallas import tpu as pltpu
from jax.sharding import PartitionSpec as P

F32, BF16 = jnp.float32, jnp.bfloat16
MESH = pl.DeviceIdType.MESH


def device(y, zh, zl, x, core):
    return (y * 4 + zh, (zl * 4 + x) * 2 + core)


def lane_index(rows):
    return lax.broadcasted_iota(jnp.int32, (rows, 128), 1)


def spread_panels(panel_in, left, g):
    for first in (0, 4):
        blocks = [
            [panel_in[g, b, :, q * 128 : (q + 1) * 128].astype(F32) for b in range(8)]
            for q in range(first, first + 4)
        ]
        rows = [jnp.concatenate([b[p][:8] for b in blocks], 0) for p in range(8)]
        rows += [jnp.concatenate([b[p][8:] for b in blocks], 0) for p in range(8)]
        lane = lane_index(32)
        for bit in (1, 2, 4, 8):
            low = (lane & bit) == 0
            new = list(rows)
            for p in range(16):
                if not p & bit:
                    lo, hi = rows[p], rows[p | bit]
                    new[p] = jnp.where(low, lo, pltpu.roll(hi, bit, 1))
                    new[p | bit] = jnp.where(low, pltpu.roll(lo, 128 - bit, 1), hi)
            rows = new
        for i in range(4):
            q = first + i
            at = ((q // 2) * 4 + g * 2 + q % 2) * 128
            left[:, at : at + 128] = jnp.concatenate([v[8 * i : 8 * i + 8] for v in rows], 0).astype(BF16)


def shift_traces(wide, right, slot, s):
    lane = lane_index(16)

    def one(g, carry):
        base = g * 32 + s * 16
        tiles = [
            jnp.concatenate([wide[pl.ds(base + p * 8 + q, 8, stride=64), :] for p in range(2)], 0)
            for q in range(8)
        ]
        for m in range(8):
            turned = [pltpu.roll(v, 16 * m, 1) if m else v for v in tiles]
            for q in range(8):
                value = turned[q]
                if m:
                    value = jnp.where(lane < 16 * m, turned[q - 1] if q else 0.0, value)
                value = value.astype(BF16)
                for h in range(2):
                    k = q + h
                    if k < 8:
                        row = pl.multiple_of((3 - k // 2) * 512 + g * 256 + h * 128 + m * 16, 16)
                        right[slot, pl.ds(row, 16), (k % 2) * 128 : (k % 2) * 128 + 128] = value
        return carry

    lax.fori_loop(0, 2, one, 0)


def convolve(left, right, slot):
    tiles = []
    for n in range(4):
        z = jnp.dot(
            left[:, : (n + 1) * 512], right[slot, (3 - n) * 512 :, :], preferred_element_type=F32
        )
        tiles += [z[:, :128], z[:, 128:]]
    for k in (8, 4, 2, 1):
        lane = lane_index(8 * k)
        turned = [pltpu.roll(z[k * 8 :], k, 1) for z in tiles]
        tiles = [
            z[: k * 8] + jnp.where(lane < k, turned[q - 1] if q else 0.0, turned[q])
            for q, z in enumerate(tiles)
        ]
    return tiles


def weigh(tiles, lower, upper):
    out = []
    for q, z in enumerate(tiles):
        t = (lane_index(8) + 128 * q).astype(F32)
        rising = jnp.clip((t - lower + 32.0) / 32.0, 0.0, 1.0)
        falling = jnp.clip((upper - t) / 32.0, 0.0, 1.0)
        out.append(rising * falling * z)
    return jnp.concatenate(out, 1)


def kernel(
    panels, traces, aperture, lo, hi, out,
    trace_raw, aperture_raw, lo_raw, hi_raw, windows, trace_wide, trace_out, window_out,
    panel_in, trace_in, window_in, wide, left, right, result_out,
    local_sem, panel_send, panel_recv, pass_send, pass_recv,
    line_send, line_recv, trace_send, trace_recv, window_send, window_recv, result_send, result_recv,
):
    shot, point = lax.axis_index("shot"), lax.axis_index("point")
    y, zh = shot // 4, shot % 4
    zl, x, core = point // 8, (point // 2) % 4, point % 2
    z = zh * 2 + zl
    half = zh // 2
    place = x * 2 + zl

    def start(source, target, send, recv, to):
        pltpu.make_async_remote_copy(
            src_ref=source, dst_ref=target, send_sem=send, recv_sem=recv, device_id=to, device_id_type=MESH
        ).start()

    def landed(ref, sem):
        pltpu.make_async_copy(ref, ref, sem).wait()

    barrier = pltpu.get_barrier_semaphore()

    def greet(to):
        pl.semaphore_signal(barrier, inc=1, device_id=to, device_id_type=MESH)

    def greet_panels(i, carry):
        greet(device(zl * 4 + x, zh, i // 4, i % 4, core))
        return carry

    def greet_line(i, carry):
        greet(device(y, core * 2 + i // 4, (i // 2) % 2, x, i % 2))
        return carry

    lax.fori_loop(0, 8, greet_panels, 0)
    lax.fori_loop(0, 8, greet_line, 0)
    for i in range(2):
        greet(device(y, core * 2 + i, zl, x, half))
    for i in range(1, 4):
        greet(device(y, zh, zl, (x + i) % 4, core))
    greet(device(y, zh, zl, x, 1 - core))

    loads = [
        pltpu.make_async_copy(source, target, local_sem.at[i])
        for i, (source, target) in enumerate(
            [(traces, trace_raw), (aperture, aperture_raw), (lo, lo_raw), (hi, hi_raw)]
        )
    ]
    for load in loads:
        load.start()

    for load in loads:
        load.wait()
    for s in range(2):
        row = trace_raw[s].astype(F32)
        for p in range(2):
            kept = row[p : p + 1, :] * aperture_raw[s : s + 1, p : p + 1].astype(F32)
            for q in range(8):
                trace_wide[s * 16 + p * 8 + q : s * 16 + p * 8 + q + 1, :] = kept[:, q * 128 : (q + 1) * 128]
    trace_out[...] = trace_wide[...].astype(BF16)
    windows[...] = jnp.zeros_like(windows)
    windows[0:2, 0:16] = lo_raw[...].astype(F32)
    windows[2:4, 0:16] = hi_raw[...].astype(F32)
    window_out[:, 0:8] = windows[...].T[:16]
    for slot in range(4):
        for g in range(2):
            right[slot, 1536 + g * 256 + 128 : 1536 + g * 256 + 256, 0:128] = jnp.zeros((128, 128), BF16)

    pl.semaphore_wait(barrier, 22)

    mine = (y // 4 == zl) & (y % 4 == x)

    def send_panel(i, carry):
        k = 4 + ((i + 1) // 2) * (2 * ((i + 1) % 2) - 1)
        start(
            panels, panel_in.at[0, place], panel_send, panel_recv.at[place],
            device((y + k) % 8, zh, y // 4, y % 4, core),
        )
        return carry

    lax.fori_loop(0, 7, send_panel, 0)

    @pl.when(mine)
    def _():
        pltpu.make_async_copy(panels, panel_in.at[0, place], panel_recv.at[place]).start()

    @pl.when(jnp.logical_not(mine))
    def _():
        start(
            panels, panel_in.at[0, place], panel_send, panel_recv.at[place], device(y, zh, y // 4, y % 4, core)
        )

    line_slot = (zh % 2) * 16 + place * 2 + (core + half) % 2
    line_sem = line_recv.at[zh % 2 * 2 + zl]
    line_target = trace_in.at[line_slot]

    def send_trace(i, carry):
        to = (z + 4 + ((i + 1) // 2) * (2 * ((i + 1) % 2) - 1)) % 8
        start(trace_out, line_target, line_send, line_sem, device(y, to // 2, to % 2, x, half))
        return carry

    lax.fori_loop(0, 7, send_trace, 0)

    @pl.when(core == half)
    def _():
        pltpu.make_async_copy(trace_out, line_target, line_sem).start()

    @pl.when(core != half)
    def _():
        start(trace_out, line_target, line_send, line_sem, device(y, zh, zl, x, half))

    for i in range(2):
        rows = window_out.at[pl.ds(i * 8, 8)]
        to = core * 2 + i
        same = (core == half) & (zh % 2 == i)
        target, sem = window_in.at[zh % 2], window_recv.at[zh % 2]

        @pl.when(same)
        def _():
            pltpu.make_async_copy(rows, target, sem).start()

        @pl.when(jnp.logical_not(same))
        def _():
            start(rows, target, window_send.at[i], sem, device(y, to, zl, x, half))

    apart = 2 * ((half + core) % 2)
    for i in range(4):
        which = (z + (apart, 1, 3, 2 - apart)[i]) % 4
        pair = trace_in.at[pl.ds(which // 2 * 16 + (x * 2 + which % 2) * 2, 2)]
        landed(pair, line_recv.at[which])
        for d in (2, 1, 3):
            start(pair, pair, trace_send, trace_recv.at[which // 2], device(y, zh, zl, (x + d) % 4, core))

    for b in range(8):
        landed(panel_in.at[0, b], panel_recv.at[b])
        start(
            panel_in.at[0, b], panel_in.at[1, b], pass_send, pass_recv, device(y, zh, zl, x, 1 - core)
        )
    spread_panels(panel_in, left, 0)
    for part in range(2):
        landed(trace_in.at[pl.ds(part * 16, 12)], trace_recv.at[part])
        wide[...] = trace_in[part * 16 : part * 16 + 16].reshape(512, 128).astype(F32)
        for s in range(2):
            shift_traces(wide, right, part * 2 + s, s)
    landed(panel_in.at[1], pass_recv)
    spread_panels(panel_in, left, 1)
    for part in range(2):
        landed(window_in.at[part], window_recv.at[part])
        for s in range(2):
            value = weigh(
                convolve(left, right, part * 2 + s),
                window_in[part, :, s : s + 1],
                window_in[part, :, 2 + s : 3 + s],
            )
            wide_rows = value.astype(BF16)
            result_out[part, s * 8 : s * 8 + 8, :] = wide_rows
        same = (core == half) & (zh % 2 == part)
        target, sem = out.at[zh % 2], result_recv.at[zh % 2]

        @pl.when(same)
        def _():
            pltpu.make_async_copy(result_out.at[part], target, sem).start()

        @pl.when(jnp.logical_not(same))
        def _():
            start(
                result_out.at[part], target, result_send.at[part], sem, device(y, core * 2 + part, zl, x, half)
            )

    for part in range(2):
        landed(out.at[part], result_recv.at[part])

    @pl.when(mine)
    def _():
        landed(panel_in.at[0, pl.ds(0, 7)], panel_send)

    @pl.when(jnp.logical_not(mine))
    def _():
        landed(panel_in.at[0], panel_send)

    @pl.when(core == half)
    def _():
        landed(trace_in.at[pl.ds(0, 7)], line_send)

    @pl.when(core != half)
    def _():
        landed(trace_in.at[pl.ds(0, 8)], line_send)

    landed(trace_in.at[pl.ds(0, 24)], trace_send)
    landed(panel_in.at[1], pass_send)
    for i in range(2):
        same = (core == half) & (zh % 2 == i)

        @pl.when(jnp.logical_not(same))
        def _():
            landed(window_in.at[i], window_send.at[i])
            landed(result_out.at[i], result_send.at[i])


def body(traces, panels, aperture, window_lo, window_hi):
    anywhere = pl.BlockSpec(memory_space=pltpu.HBM)
    out = pl.pallas_call(
        kernel,
        out_shape=pltpu.VMEM((2, 16, 1024), BF16),
        in_specs=[anywhere] * 5,
        out_specs=pl.BlockSpec(memory_space=pltpu.VMEM),
        scratch_shapes=[
            pltpu.VMEM((2, 2, 1024), BF16),
            pltpu.VMEM((2, 2), jnp.int32),
            pltpu.VMEM((2, 16), jnp.int32),
            pltpu.VMEM((2, 16), jnp.int32),
            pltpu.VMEM((8, 128), F32),
            pltpu.VMEM((32, 128), F32),
            pltpu.VMEM((32, 128), BF16),
            pltpu.VMEM((16, 128), F32),
            pltpu.VMEM((2, 8, 16, 1024), BF16),
            pltpu.VMEM((32, 32, 128), BF16),
            pltpu.VMEM((2, 8, 128), F32),
            pltpu.VMEM((512, 128), F32),
            pltpu.VMEM((128, 2048), BF16),
            pltpu.VMEM((4, 2048, 256), BF16),
            pltpu.VMEM((2, 16, 1024), BF16),
            pltpu.SemaphoreType.DMA((4,)),
            pltpu.SemaphoreType.DMA,
            pltpu.SemaphoreType.DMA((8,)),
            pltpu.SemaphoreType.DMA,
            pltpu.SemaphoreType.DMA,
            pltpu.SemaphoreType.DMA,
            pltpu.SemaphoreType.DMA((4,)),
            pltpu.SemaphoreType.DMA,
            pltpu.SemaphoreType.DMA((2,)),
            pltpu.SemaphoreType.DMA((2,)),
            pltpu.SemaphoreType.DMA((2,)),
            pltpu.SemaphoreType.DMA((2,)),
            pltpu.SemaphoreType.DMA((2,)),
        ],
        compiler_params=pltpu.CompilerParams(
            collective_id=0, has_side_effects=True, vmem_limit_bytes=60 << 20
        ),
    )(panels.reshape(16, 1024), traces, aperture, window_lo.T, window_hi.T)
    return out.reshape(2, 2, 8, 1024).transpose(0, 2, 1, 3).reshape(16, 2, 1024)


def solution(mesh):
    in_specs = (
        P("shot", "point", None),
        P("point", "shot", None),
        P("shot", "point"),
        P("point", "shot"),
        P("point", "shot"),
    )
    out_specs = P("point", "shot", None)
    return jax.shard_map(body, mesh=mesh, in_specs=in_specs, out_specs=out_specs, check_vma=False)
```

```python
import jax
import jax.numpy as jnp
from jax import lax
from jax.experimental import pallas as pl
from jax.experimental.pallas import tpu as pltpu
from jax.sharding import PartitionSpec as P

F32, BF16 = jnp.float32, jnp.bfloat16
MESH = pl.DeviceIdType.MESH


def device(y, zh, zl, x, core):
    return (y * 4 + zh, (zl * 4 + x) * 2 + core)


def lane_index(rows):
    return lax.broadcasted_iota(jnp.int32, (rows, 128), 1)


def spread_panels(panel_in, left, g):
    for first in (0, 4):
        blocks = [
            [panel_in[g, b, :, q * 128 : (q + 1) * 128].astype(F32) for b in range(8)]
            for q in range(first, first + 4)
        ]
        rows = [jnp.concatenate([b[p][:8] for b in blocks], 0) for p in range(8)]
        rows += [jnp.concatenate([b[p][8:] for b in blocks], 0) for p in range(8)]
        lane = lane_index(32)
        for bit in (1, 2, 4, 8):
            low = (lane & bit) == 0
            new = list(rows)
            for p in range(16):
                if not p & bit:
                    lo, hi = rows[p], rows[p | bit]
                    new[p] = jnp.where(low, lo, pltpu.roll(hi, bit, 1))
                    new[p | bit] = jnp.where(low, pltpu.roll(lo, 128 - bit, 1), hi)
            rows = new
        for i in range(4):
            q = first + i
            at = ((q // 2) * 4 + g * 2 + q % 2) * 128
            left[:, at : at + 128] = jnp.concatenate([v[8 * i : 8 * i + 8] for v in rows], 0).astype(BF16)


def shift_traces(wide, right, slot, s):
    lane = lane_index(16)

    for g in range(2):
        base = g * 32 + s * 16
        tiles = [
            jnp.concatenate([wide[pl.ds(base + p * 8 + q, 8, stride=64), :] for p in range(2)], 0)
            for q in range(8)
        ]
        for m in range(8):
            turned = [pltpu.roll(v, 16 * m, 1) if m else v for v in tiles]
            for q in range(8):
                value = turned[q]
                if m:
                    value = jnp.where(lane < 16 * m, turned[q - 1] if q else 0.0, value)
                value = value.astype(BF16)
                for h in range(2):
                    k = q + h
                    if k < 8:
                        row = (3 - k // 2) * 512 + g * 256 + h * 128 + m * 16
                        right[slot, row : row + 16, (k % 2) * 128 : (k % 2) * 128 + 128] = value


def convolve(left, right, slot):
    tiles = []
    for n in range(4):
        z = jnp.dot(
            left[:, : (n + 1) * 512], right[slot, (3 - n) * 512 :, :], preferred_element_type=F32
        )
        tiles += [z[:, :128], z[:, 128:]]
    for k in (8, 4, 2, 1):
        lane = lane_index(8 * k)
        turned = [pltpu.roll(z[k * 8 :], k, 1) for z in tiles]
        tiles = [
            z[: k * 8] + jnp.where(lane < k, turned[q - 1] if q else 0.0, turned[q])
            for q, z in enumerate(tiles)
        ]
    return tiles


def weigh(tiles, lower, upper):
    out = []
    for q, z in enumerate(tiles):
        t = (lane_index(8) + 128 * q).astype(F32)
        rising = jnp.clip((t - lower + 32.0) / 32.0, 0.0, 1.0)
        falling = jnp.clip((upper - t) / 32.0, 0.0, 1.0)
        out.append(rising * falling * z)
    return jnp.concatenate(out, 1)


def kernel(
    panels, traces, aperture, lo, hi, out,
    trace_raw, aperture_raw, lo_raw, hi_raw, windows, trace_wide, trace_out, window_out,
    panel_in, trace_in, window_in, wide, left, right, result_out,
    local_sem, panel_send, panel_recv, pass_send, pass_recv,
    line_send, line_recv, trace_send, trace_recv, window_send, window_recv, result_send, result_recv,
):
    shot, point = lax.axis_index("shot"), lax.axis_index("point")
    y, zh = shot // 4, shot % 4
    zl, x, core = point // 8, (point // 2) % 4, point % 2
    z = zh * 2 + zl
    half = zh // 2
    place = x * 2 + zl

    def start(source, target, send, recv, to):
        pltpu.make_async_remote_copy(
            src_ref=source, dst_ref=target, send_sem=send, recv_sem=recv, device_id=to, device_id_type=MESH
        ).start()

    def landed(ref, sem):
        pltpu.make_async_copy(ref, ref, sem).wait()

    barrier = pltpu.get_barrier_semaphore()

    def greet(to):
        pl.semaphore_signal(barrier, inc=1, device_id=to, device_id_type=MESH)

    def greet_panels(i, carry):
        greet(device(zl * 4 + x, zh, i // 4, i % 4, core))
        return carry

    def greet_line(i, carry):
        greet(device(y, core * 2 + i // 4, (i // 2) % 2, x, i % 2))
        return carry

    lax.fori_loop(0, 8, greet_panels, 0)
    lax.fori_loop(0, 8, greet_line, 0)
    for i in range(2):
        greet(device(y, core * 2 + i, zl, x, half))
    for i in range(1, 4):
        greet(device(y, zh, zl, (x + i) % 4, core))
    greet(device(y, zh, zl, x, 1 - core))

    loads = [
        pltpu.make_async_copy(source, target, local_sem.at[i])
        for i, (source, target) in enumerate(
            [(traces, trace_raw), (aperture, aperture_raw), (lo, lo_raw), (hi, hi_raw)]
        )
    ]
    for load in loads:
        load.start()

    for load in loads:
        load.wait()
    for s in range(2):
        row = trace_raw[s].astype(F32)
        for p in range(2):
            kept = row[p : p + 1, :] * aperture_raw[s : s + 1, p : p + 1].astype(F32)
            for q in range(8):
                trace_wide[s * 16 + p * 8 + q : s * 16 + p * 8 + q + 1, :] = kept[:, q * 128 : (q + 1) * 128]
    trace_out[...] = trace_wide[...].astype(BF16)
    windows[...] = jnp.zeros_like(windows)
    windows[0:2, 0:16] = lo_raw[...].astype(F32)
    windows[2:4, 0:16] = hi_raw[...].astype(F32)
    window_out[:, 0:8] = windows[...].T[:16]
    for slot in range(4):
        for g in range(2):
            right[slot, 1536 + g * 256 + 128 : 1536 + g * 256 + 256, 0:128] = jnp.zeros((128, 128), BF16)

    pl.semaphore_wait(barrier, 22)

    mine = (y // 4 == zl) & (y % 4 == x)

    def send_panel(i, carry):
        k = 4 + ((i + 1) // 2) * (2 * ((i + 1) % 2) - 1)
        start(
            panels, panel_in.at[0, place], panel_send, panel_recv.at[place],
            device((y + k) % 8, zh, y // 4, y % 4, core),
        )
        return carry

    lax.fori_loop(0, 7, send_panel, 0)

    @pl.when(mine)
    def _():
        pltpu.make_async_copy(panels, panel_in.at[0, place], panel_recv.at[place]).start()

    @pl.when(jnp.logical_not(mine))
    def _():
        start(
            panels, panel_in.at[0, place], panel_send, panel_recv.at[place], device(y, zh, y // 4, y % 4, core)
        )

    line_slot = (zh % 2) * 16 + place * 2 + (core + half) % 2
    line_sem = line_recv.at[zh % 2 * 2 + zl]
    line_target = trace_in.at[line_slot]

    def send_trace(i, carry):
        to = (z + 4 + ((i + 1) // 2) * (2 * ((i + 1) % 2) - 1)) % 8
        start(trace_out, line_target, line_send, line_sem, device(y, to // 2, to % 2, x, half))
        return carry

    lax.fori_loop(0, 7, send_trace, 0)

    @pl.when(core == half)
    def _():
        pltpu.make_async_copy(trace_out, line_target, line_sem).start()

    @pl.when(core != half)
    def _():
        start(trace_out, line_target, line_send, line_sem, device(y, zh, zl, x, half))

    for i in range(2):
        rows = window_out.at[pl.ds(i * 8, 8)]
        to = core * 2 + i
        same = (core == half) & (zh % 2 == i)
        target, sem = window_in.at[zh % 2], window_recv.at[zh % 2]

        @pl.when(same)
        def _():
            pltpu.make_async_copy(rows, target, sem).start()

        @pl.when(jnp.logical_not(same))
        def _():
            start(rows, target, window_send.at[i], sem, device(y, to, zl, x, half))

    apart = 2 * ((half + core) % 2)
    for i in range(4):
        which = (z + (apart, 1, 3, 2 - apart)[i]) % 4
        pair = trace_in.at[pl.ds(which // 2 * 16 + (x * 2 + which % 2) * 2, 2)]
        landed(pair, line_recv.at[which])
        for d in (2, 1, 3):
            start(pair, pair, trace_send, trace_recv.at[which // 2], device(y, zh, zl, (x + d) % 4, core))

    for b in range(8):
        landed(panel_in.at[0, b], panel_recv.at[b])
        start(
            panel_in.at[0, b], panel_in.at[1, b], pass_send, pass_recv, device(y, zh, zl, x, 1 - core)
        )
    spread_panels(panel_in, left, 0)
    landed(panel_in.at[1], pass_recv)
    spread_panels(panel_in, left, 1)
    for part in range(2):
        landed(window_in.at[part], window_recv.at[part])
        landed(trace_in.at[pl.ds(part * 16, 12)], trace_recv.at[part])
        wide[part] = trace_in[part * 16 : part * 16 + 16].reshape(512, 128).astype(F32)
        for s in range(2):
            shift_traces(wide.at[part], right, part * 2 + s, s)
            value = weigh(
                convolve(left, right, part * 2 + s),
                window_in[part, :, s : s + 1],
                window_in[part, :, 2 + s : 3 + s],
            )
            wide_rows = value.astype(BF16)
            result_out[part, s * 8 : s * 8 + 8, :] = wide_rows
        same = (core == half) & (zh % 2 == part)
        target, sem = out.at[zh % 2], result_recv.at[zh % 2]

        @pl.when(same)
        def _():
            pltpu.make_async_copy(result_out.at[part], target, sem).start()

        @pl.when(jnp.logical_not(same))
        def _():
            start(
                result_out.at[part], target, result_send.at[part], sem, device(y, core * 2 + part, zl, x, half)
            )

    for part in range(2):
        landed(out.at[part], result_recv.at[part])

    @pl.when(mine)
    def _():
        landed(panel_in.at[0, pl.ds(0, 7)], panel_send)

    @pl.when(jnp.logical_not(mine))
    def _():
        landed(panel_in.at[0], panel_send)

    @pl.when(core == half)
    def _():
        landed(trace_in.at[pl.ds(0, 7)], line_send)

    @pl.when(core != half)
    def _():
        landed(trace_in.at[pl.ds(0, 8)], line_send)

    landed(trace_in.at[pl.ds(0, 24)], trace_send)
    landed(panel_in.at[1], pass_send)
    for i in range(2):
        same = (core == half) & (zh % 2 == i)

        @pl.when(jnp.logical_not(same))
        def _():
            landed(window_in.at[i], window_send.at[i])
            landed(result_out.at[i], result_send.at[i])


def body(traces, panels, aperture, window_lo, window_hi):
    anywhere = pl.BlockSpec(memory_space=pltpu.HBM)
    out = pl.pallas_call(
        kernel,
        out_shape=pltpu.VMEM((2, 16, 1024), BF16),
        in_specs=[anywhere] * 5,
        out_specs=pl.BlockSpec(memory_space=pltpu.VMEM),
        scratch_shapes=[
            pltpu.VMEM((2, 2, 1024), BF16),
            pltpu.VMEM((2, 2), jnp.int32),
            pltpu.VMEM((2, 16), jnp.int32),
            pltpu.VMEM((2, 16), jnp.int32),
            pltpu.VMEM((8, 128), F32),
            pltpu.VMEM((32, 128), F32),
            pltpu.VMEM((32, 128), BF16),
            pltpu.VMEM((16, 128), F32),
            pltpu.VMEM((2, 8, 16, 1024), BF16),
            pltpu.VMEM((32, 32, 128), BF16),
            pltpu.VMEM((2, 8, 128), F32),
            pltpu.VMEM((2, 512, 128), F32),
            pltpu.VMEM((128, 2048), BF16),
            pltpu.VMEM((4, 2048, 256), BF16),
            pltpu.VMEM((2, 16, 1024), BF16),
            pltpu.SemaphoreType.DMA((4,)),
            pltpu.SemaphoreType.DMA,
            pltpu.SemaphoreType.DMA((8,)),
            pltpu.SemaphoreType.DMA,
            pltpu.SemaphoreType.DMA,
            pltpu.SemaphoreType.DMA,
            pltpu.SemaphoreType.DMA((4,)),
            pltpu.SemaphoreType.DMA,
            pltpu.SemaphoreType.DMA((2,)),
            pltpu.SemaphoreType.DMA((2,)),
            pltpu.SemaphoreType.DMA((2,)),
            pltpu.SemaphoreType.DMA((2,)),
            pltpu.SemaphoreType.DMA((2,)),
        ],
        compiler_params=pltpu.CompilerParams(
            collective_id=0, has_side_effects=True, vmem_limit_bytes=60 << 20
        ),
    )(panels.reshape(16, 1024), traces, aperture, window_lo.T, window_hi.T)
    return out.reshape(2, 2, 8, 1024).transpose(0, 2, 1, 3).reshape(16, 2, 1024)


def solution(mesh):
    in_specs = (
        P("shot", "point", None),
        P("point", "shot", None),
        P("shot", "point"),
        P("point", "shot"),
        P("point", "shot"),
    )
    out_specs = P("point", "shot", None)
    return jax.shard_map(body, mesh=mesh, in_specs=in_specs, out_specs=out_specs, check_vma=False)
```

```python
import jax
import jax.numpy as jnp
from jax import lax
from jax.experimental import pallas as pl
from jax.experimental.pallas import tpu as pltpu
from jax.sharding import PartitionSpec as P

F32, BF16 = jnp.float32, jnp.bfloat16
MESH = pl.DeviceIdType.MESH


def device(y, zh, zl, x, core):
    return (y * 4 + zh, (zl * 4 + x) * 2 + core)


def lane_index(rows):
    return lax.broadcasted_iota(jnp.int32, (rows, 128), 1)


def spread_panels(panel_in, left, g):
    for first in (0, 4):
        rows = [
            jnp.concatenate([panel_in[g, b, :, q * 128 : (q + 1) * 128] for q in range(first, first + 4)], 0)
            for b in range(8)
        ]
        lane = lane_index(64)
        for bit in (1, 2, 4):
            low = (lane & bit) == 0
            new = list(rows)
            for p in range(8):
                if not p & bit:
                    lo, hi = rows[p], rows[p | bit]
                    new[p] = jnp.where(low, lo, pltpu.roll(hi, bit, 1))
                    new[p | bit] = jnp.where(low, pltpu.roll(lo, 128 - bit, 1), hi)
            rows = new
        low = (lane_index(8) & 8) == 0
        for i in range(4):
            q = first + i
            lower, upper = [], []
            for v in rows:
                v = v[16 * i : 16 * i + 16].astype(F32)
                lower.append(jnp.where(low, v[:8], pltpu.roll(v[8:], 8, 1)))
                upper.append(jnp.where(low, pltpu.roll(v[:8], 120, 1), v[8:]))
            at = ((q // 2) * 4 + g * 2 + q % 2) * 128
            left[:, at : at + 128] = jnp.concatenate(lower + upper, 0).astype(BF16)


def shift_traces(wide, right, slot, s):
    lane = lane_index(16)

    for g in range(2):
        base = g * 32 + s * 16
        tiles = [
            jnp.concatenate([wide[pl.ds(base + p * 8 + q, 8, stride=64), :] for p in range(2)], 0)
            for q in range(8)
        ]
        for m in range(8):
            turned = [pltpu.roll(v, 16 * m, 1) if m else v for v in tiles]
            for q in range(8):
                value = turned[q]
                if m:
                    value = jnp.where(lane < 16 * m, turned[q - 1] if q else 0.0, value)
                value = value.astype(BF16)
                for h in range(2):
                    k = q + h
                    if k < 8:
                        row = (3 - k // 2) * 512 + g * 256 + h * 128 + m * 16
                        right[slot, row : row + 16, (k % 2) * 128 : (k % 2) * 128 + 128] = value


def convolve(left, right, slot):
    tiles = []
    for n in range(4):
        z = jnp.dot(
            left[:, : (n + 1) * 512], right[slot, (3 - n) * 512 :, :], preferred_element_type=F32
        )
        tiles += [z[:, :128], z[:, 128:]]
    for k in (8, 4, 2, 1):
        lane = lane_index(8 * k)
        turned = [pltpu.roll(z[k * 8 :], k, 1) for z in tiles]
        tiles = [
            z[: k * 8] + jnp.where(lane < k, turned[q - 1] if q else 0.0, turned[q])
            for q, z in enumerate(tiles)
        ]
    return tiles


def weigh(tiles, lower, upper):
    out = []
    for q, z in enumerate(tiles):
        t = (lane_index(8) + 128 * q).astype(F32)
        rising = jnp.clip((t - lower + 32.0) / 32.0, 0.0, 1.0)
        falling = jnp.clip((upper - t) / 32.0, 0.0, 1.0)
        out.append(rising * falling * z)
    return jnp.concatenate(out, 1)


def kernel(
    panels, traces, aperture, lo, hi, out,
    trace_raw, aperture_raw, lo_raw, hi_raw, windows, trace_wide, trace_out, window_out,
    panel_in, trace_in, window_in, wide, left, right, result_out,
    local_sem, panel_send, panel_recv, pass_send, pass_recv,
    line_send, line_recv, trace_send, trace_recv, window_send, window_recv, result_send, result_recv,
):
    shot, point = lax.axis_index("shot"), lax.axis_index("point")
    y, zh = shot // 4, shot % 4
    zl, x, core = point // 8, (point // 2) % 4, point % 2
    z = zh * 2 + zl
    half = zh // 2
    place = x * 2 + zl

    def start(source, target, send, recv, to):
        pltpu.make_async_remote_copy(
            src_ref=source, dst_ref=target, send_sem=send, recv_sem=recv, device_id=to, device_id_type=MESH
        ).start()

    def landed(ref, sem):
        pltpu.make_async_copy(ref, ref, sem).wait()

    barrier = pltpu.get_barrier_semaphore()

    def greet(to):
        pl.semaphore_signal(barrier, inc=1, device_id=to, device_id_type=MESH)

    def greet_panels(i, carry):
        greet(device(zl * 4 + x, zh, i // 4, i % 4, core))
        return carry

    def greet_line(i, carry):
        greet(device(y, core * 2 + i // 4, (i // 2) % 2, x, i % 2))
        return carry

    lax.fori_loop(0, 8, greet_panels, 0)
    lax.fori_loop(0, 8, greet_line, 0)
    for i in range(2):
        greet(device(y, core * 2 + i, zl, x, half))
    for i in range(1, 4):
        greet(device(y, zh, zl, (x + i) % 4, core))
    greet(device(y, zh, zl, x, 1 - core))

    loads = [
        pltpu.make_async_copy(source, target, local_sem.at[i])
        for i, (source, target) in enumerate(
            [(traces, trace_raw), (aperture, aperture_raw), (lo, lo_raw), (hi, hi_raw)]
        )
    ]
    for load in loads:
        load.start()

    for load in loads:
        load.wait()
    for s in range(2):
        row = trace_raw[s].astype(F32)
        for p in range(2):
            kept = row[p : p + 1, :] * aperture_raw[s : s + 1, p : p + 1].astype(F32)
            for q in range(8):
                trace_wide[s * 16 + p * 8 + q : s * 16 + p * 8 + q + 1, :] = kept[:, q * 128 : (q + 1) * 128]
    trace_out[...] = trace_wide[...].astype(BF16)
    windows[...] = jnp.zeros_like(windows)
    windows[0:2, 0:16] = lo_raw[...].astype(F32)
    windows[2:4, 0:16] = hi_raw[...].astype(F32)
    window_out[:, 0:8] = windows[...].T[:16]
    for slot in range(4):
        for g in range(2):
            right[slot, 1536 + g * 256 + 128 : 1536 + g * 256 + 256, 0:128] = jnp.zeros((128, 128), BF16)

    pl.semaphore_wait(barrier, 22)

    mine = (y // 4 == zl) & (y % 4 == x)

    def send_panel(i, carry):
        k = 4 + ((i + 1) // 2) * (2 * ((i + 1) % 2) - 1)
        start(
            panels, panel_in.at[0, place], panel_send, panel_recv.at[place],
            device((y + k) % 8, zh, y // 4, y % 4, core),
        )
        return carry

    lax.fori_loop(0, 7, send_panel, 0)

    @pl.when(mine)
    def _():
        pltpu.make_async_copy(panels, panel_in.at[0, place], panel_recv.at[place]).start()

    @pl.when(jnp.logical_not(mine))
    def _():
        start(
            panels, panel_in.at[0, place], panel_send, panel_recv.at[place], device(y, zh, y // 4, y % 4, core)
        )

    line_slot = (zh % 2) * 16 + place * 2 + (core + half) % 2
    line_sem = line_recv.at[zh % 2 * 2 + zl]
    line_target = trace_in.at[line_slot]

    def send_trace(i, carry):
        to = (z + 4 + ((i + 1) // 2) * (2 * ((i + 1) % 2) - 1)) % 8
        start(trace_out, line_target, line_send, line_sem, device(y, to // 2, to % 2, x, half))
        return carry

    lax.fori_loop(0, 7, send_trace, 0)

    @pl.when(core == half)
    def _():
        pltpu.make_async_copy(trace_out, line_target, line_sem).start()

    @pl.when(core != half)
    def _():
        start(trace_out, line_target, line_send, line_sem, device(y, zh, zl, x, half))

    for i in range(2):
        rows = window_out.at[pl.ds(i * 8, 8)]
        to = core * 2 + i
        same = (core == half) & (zh % 2 == i)
        target, sem = window_in.at[zh % 2], window_recv.at[zh % 2]

        @pl.when(same)
        def _():
            pltpu.make_async_copy(rows, target, sem).start()

        @pl.when(jnp.logical_not(same))
        def _():
            start(rows, target, window_send.at[i], sem, device(y, to, zl, x, half))

    apart = 2 * ((half + core) % 2)
    for i in range(4):
        which = (z + (apart, 1, 3, 2 - apart)[i]) % 4
        pair = trace_in.at[pl.ds(which // 2 * 16 + (x * 2 + which % 2) * 2, 2)]
        landed(pair, line_recv.at[which])
        for d in (2, 1, 3):
            start(pair, pair, trace_send, trace_recv.at[which // 2], device(y, zh, zl, (x + d) % 4, core))

    for b in range(8):
        landed(panel_in.at[0, b], panel_recv.at[b])
        start(
            panel_in.at[0, b], panel_in.at[1, b], pass_send, pass_recv, device(y, zh, zl, x, 1 - core)
        )
    spread_panels(panel_in, left, 0)
    landed(panel_in.at[1], pass_recv)
    spread_panels(panel_in, left, 1)
    for part in range(2):
        landed(window_in.at[part], window_recv.at[part])
        landed(trace_in.at[pl.ds(part * 16, 12)], trace_recv.at[part])
        wide[part] = trace_in[part * 16 : part * 16 + 16].reshape(512, 128).astype(F32)
        for s in range(2):
            shift_traces(wide.at[part], right, part * 2 + s, s)
            value = weigh(
                convolve(left, right, part * 2 + s),
                window_in[part, :, s : s + 1],
                window_in[part, :, 2 + s : 3 + s],
            )
            wide_rows = value.astype(BF16)
            result_out[part, s * 8 : s * 8 + 8, :] = wide_rows
        same = (core == half) & (zh % 2 == part)
        target, sem = out.at[zh % 2], result_recv.at[zh % 2]

        @pl.when(same)
        def _():
            pltpu.make_async_copy(result_out.at[part], target, sem).start()

        @pl.when(jnp.logical_not(same))
        def _():
            start(
                result_out.at[part], target, result_send.at[part], sem, device(y, core * 2 + part, zl, x, half)
            )

    for part in range(2):
        landed(out.at[part], result_recv.at[part])

    @pl.when(mine)
    def _():
        landed(panel_in.at[0, pl.ds(0, 7)], panel_send)

    @pl.when(jnp.logical_not(mine))
    def _():
        landed(panel_in.at[0], panel_send)

    @pl.when(core == half)
    def _():
        landed(trace_in.at[pl.ds(0, 7)], line_send)

    @pl.when(core != half)
    def _():
        landed(trace_in.at[pl.ds(0, 8)], line_send)

    landed(trace_in.at[pl.ds(0, 24)], trace_send)
    landed(panel_in.at[1], pass_send)
    for i in range(2):
        same = (core == half) & (zh % 2 == i)

        @pl.when(jnp.logical_not(same))
        def _():
            landed(window_in.at[i], window_send.at[i])
            landed(result_out.at[i], result_send.at[i])


def body(traces, panels, aperture, window_lo, window_hi):
    anywhere = pl.BlockSpec(memory_space=pltpu.HBM)
    out = pl.pallas_call(
        kernel,
        out_shape=pltpu.VMEM((2, 16, 1024), BF16),
        in_specs=[anywhere] * 5,
        out_specs=pl.BlockSpec(memory_space=pltpu.VMEM),
        scratch_shapes=[
            pltpu.VMEM((2, 2, 1024), BF16),
            pltpu.VMEM((2, 2), jnp.int32),
            pltpu.VMEM((2, 16), jnp.int32),
            pltpu.VMEM((2, 16), jnp.int32),
            pltpu.VMEM((8, 128), F32),
            pltpu.VMEM((32, 128), F32),
            pltpu.VMEM((32, 128), BF16),
            pltpu.VMEM((16, 128), F32),
            pltpu.VMEM((2, 8, 16, 1024), BF16),
            pltpu.VMEM((32, 32, 128), BF16),
            pltpu.VMEM((2, 8, 128), F32),
            pltpu.VMEM((2, 512, 128), F32),
            pltpu.VMEM((128, 2048), BF16),
            pltpu.VMEM((4, 2048, 256), BF16),
            pltpu.VMEM((2, 16, 1024), BF16),
            pltpu.SemaphoreType.DMA((4,)),
            pltpu.SemaphoreType.DMA,
            pltpu.SemaphoreType.DMA((8,)),
            pltpu.SemaphoreType.DMA,
            pltpu.SemaphoreType.DMA,
            pltpu.SemaphoreType.DMA,
            pltpu.SemaphoreType.DMA((4,)),
            pltpu.SemaphoreType.DMA,
            pltpu.SemaphoreType.DMA((2,)),
            pltpu.SemaphoreType.DMA((2,)),
            pltpu.SemaphoreType.DMA((2,)),
            pltpu.SemaphoreType.DMA((2,)),
            pltpu.SemaphoreType.DMA((2,)),
        ],
        compiler_params=pltpu.CompilerParams(
            collective_id=0, has_side_effects=True, vmem_limit_bytes=60 << 20
        ),
    )(panels.reshape(16, 1024), traces, aperture, window_lo.T, window_hi.T)
    return out.reshape(2, 2, 8, 1024).transpose(0, 2, 1, 3).reshape(16, 2, 1024)


def solution(mesh):
    in_specs = (
        P("shot", "point", None),
        P("point", "shot", None),
        P("shot", "point"),
        P("point", "shot"),
        P("point", "shot"),
    )
    out_specs = P("point", "shot", None)
    return jax.shard_map(body, mesh=mesh, in_specs=in_specs, out_specs=out_specs, check_vma=False)
```
